512 devices in a mesh: section: 16 (over y, core), blk: 32 (over x, z).
Axes of the slice: x: 4, y: 8, z: 8, core: 2. Of those that a mesh axis runs over, the one named last changes fastest.
Arguments:
- residual: float32 [24576, 32, 128], P(('section', 'blk')), may hold values from -6 to 6
- kin_inverse: float32 [24576, 32, 32], P(('section', 'blk'))
- cell_weight: float32 [24576, 128], P(('section', 'blk')), may hold values from 0.5 to 1
- upwind_frac: float32 [24576, 4, 128], P(('section', 'blk')), may hold values from 0.2 to 0.7
- block_level: int32 [24576], P(('section', 'blk')), may hold values from 0 to 5, as said below
- send_in: int32 [512, 5, 32], P(('section', 'blk')), may hold values from 0 to 48, as said below
- send_down: int32 [512, 5, 32], P(('section', 'blk')), may hold values from 0 to 48, as said below
- upwind_slot: int32 [24576, 4], P(('section', 'blk')), may hold values from 0 to 368, as said below
Outputs:
- newton_step: float32 [24576, 32, 128], P(('section', 'blk'))
The draws below stay inside these ranges and needn't reach their ends.
Inputs may be any that keep to these rules, and one draw needn't show every extreme that they name: `block_level`: on each device the blocks of levels 0 to 5 number 48 * 8 / 24, 6 / 24, 4 / 24, 3 / 24, 2 / 24 and 1 / 24 in some cyclic order of the levels, so one level holds 16 blocks of every device. `send_in`: an entry other than 48 names a block of level l on the sending device, for entry [d, l, i]. About half of the entries are none; for every section and level some device receives a block from every device of its section. `send_down`: as send_in, for the owner i of the next section. The last section sends none; for every other section and level some device of the next section receives a block from every device of the sending section. `upwind_slot`: every source of a block has a lower level than the block (a slot of send level l counts as level l), and a slot that is named holds a block; blocks of level 0 have none.
All inputs are finite; a program needn't handle non-finite values.
Results may differ from the reference program's by a relative error of at most 0.0001.
Values sent between devices are 32-bit elements; how exact they have to be, the bound alone decides.
A program may use at most 64 MiB of HBM per device.

```python
import math
import jax
import jax.numpy as jnp
import numpy as np
from jax import lax

SPEC = 32
CELLS = 128
LEVELS = 6
UPW = 4
BLK_DEV = 48
BLOCKS = 24576
N_SECTION = 16
N_BLK = 32


def routing(key):
    devices = N_SECTION * N_BLK
    rounds = LEVELS - 1
    keys = jax.random.split(key, 10)
    pattern = np.repeat(np.arange(LEVELS), np.array([8, 6, 4, 3, 2, 1]) * (BLK_DEV // 24))
    offset = jax.random.randint(keys[0], (devices, 1), 0, LEVELS)
    cyclic = (jnp.asarray(pattern, jnp.int32)[None, :] + offset) % LEVELS
    local_iota = jnp.arange(BLK_DEV, dtype=jnp.int32)
    shuffle = jax.random.randint(keys[1], (devices, BLK_DEV), 0, 1 << 20) * BLK_DEV + local_iota[None, :]
    order = jnp.argsort(shuffle, axis=1)
    levels = jnp.take_along_axis(cyclic, order, axis=1).astype(jnp.int32)
    round_ids = jnp.arange(rounds, dtype=jnp.int32)
    eligible = levels[:, None, None, :] == round_ids[None, :, None, None]
    section_of = (jnp.arange(devices, dtype=jnp.int32) // N_BLK)[:, None, None]
    peer_ids = jnp.arange(N_BLK, dtype=jnp.int32)[None, None, :]

    def pick(key_pick, key_fill, key_star):
        scores = jax.random.randint(key_pick, (devices, rounds, N_BLK, BLK_DEV), 0, 1 << 20) * BLK_DEV + local_iota
        chosen = jnp.argmax(jnp.where(eligible, scores, -1), axis=-1).astype(jnp.int32)
        coin = jax.random.randint(key_fill, (devices, rounds, N_BLK), 0, 2) == 1
        star = jax.random.randint(key_star, (N_SECTION, rounds), 0, N_BLK)
        forced = star[section_of[:, 0, 0]][:, :, None] == peer_ids
        return jnp.where(coin | forced, chosen, BLK_DEV).astype(jnp.int32)
    send_in = pick(keys[2], keys[3], keys[4])
    send_down = jnp.where(section_of == N_SECTION - 1, BLK_DEV, pick(keys[5], keys[6], keys[7])).astype(jnp.int32)
    in_view = send_in.reshape(N_SECTION, N_BLK, rounds, N_BLK).transpose(0, 3, 2, 1)
    filled_in = (in_view != BLK_DEV).reshape(devices, rounds * N_BLK)
    down_view = send_down.reshape(N_SECTION, N_BLK, rounds, N_BLK).transpose(0, 3, 2, 1)
    down_view = jnp.concatenate([jnp.full((1, N_BLK, rounds, N_BLK), BLK_DEV, jnp.int32), down_view[:-1]], axis=0)
    filled_down = (down_view != BLK_DEV).reshape(devices, rounds * N_BLK)
    filled = jnp.concatenate([filled_in, filled_down], axis=1)
    candidates = 2 * rounds * N_BLK
    cand_level = jnp.tile(jnp.repeat(round_ids, N_BLK), 2)
    cand_iota = jnp.arange(candidates, dtype=jnp.int32)
    usable = filled[:, None, :] & (cand_level[None, None, :] < levels[:, :, None])
    remote_scores = jax.random.randint(keys[8], (devices, BLK_DEV, candidates), 0, 1 << 20) * candidates + cand_iota
    masked = jnp.where(usable, remote_scores, -1 - cand_iota)
    top_values, top_index = lax.top_k(masked, UPW - 1)
    remote_slot = jnp.where(top_values >= 0, BLK_DEV + 1 + top_index, BLK_DEV)
    lower = levels[:, None, :] < levels[:, :, None]
    local_scores = jax.random.randint(keys[9], (devices, BLK_DEV, BLK_DEV), 0, 1 << 20) * BLK_DEV + local_iota
    local_pick = jnp.argmax(jnp.where(lower, local_scores, -1), axis=-1)
    local_slot = jnp.where(jnp.any(lower, axis=-1), local_pick, BLK_DEV)
    upwind = jnp.concatenate([local_slot[:, :, None], remote_slot], axis=-1).reshape(devices * BLK_DEV, UPW)
    return (levels.reshape(-1), send_in, send_down, upwind.astype(jnp.int32))


def draw_block_level(key, part):
    return routing(jax.random.fold_in(key, 11))[0]


def draw_send_in(key, part):
    return routing(jax.random.fold_in(key, 11))[1]


def draw_send_down(key, part):
    return routing(jax.random.fold_in(key, 11))[2]


def draw_upwind_slot(key, part):
    return routing(jax.random.fold_in(key, 11))[3]


def draw_kin_inverse(key, part):
    key_diag, key_off = jax.random.split(key)
    count = BLK_DEV * N_SECTION * N_BLK
    diagonal = jax.random.uniform(key_diag, (count, SPEC), jnp.float32, 0.6, 1.0)
    spread = jax.random.normal(key_off, (count, SPEC, SPEC), jnp.float32) * (0.35 / math.sqrt(SPEC))
    return spread + diagonal[:, :, None] * jnp.eye(SPEC, dtype=jnp.float32)[None, :, :]


def block_levels(key, dims, cuts, least, high):
    factor_of = 1.0
    for position, shards_of in cuts:
        heights = jax.random.uniform(jax.random.fold_in(jax.random.fold_in(key, 6), position), (shards_of,), jnp.float32, least / len(cuts), high / len(cuts))
        factor_of = factor_of * jnp.repeat(jnp.exp(heights), dims[position] // shards_of).reshape((-1,) + (1,) * (len(dims) - 1 - position))
    return factor_of


def noise(key, dims, scale, limit, shards=(), kind=jnp.bfloat16):
    drawn = scale * jax.random.normal(key, dims, jnp.float32)
    if shards:
        drawn = drawn * block_levels(key, dims, shards, -0.22, 0.18)
    return jnp.clip(drawn, -limit, limit).astype(kind)


def setup_inputs(seed: int = 0) -> dict:
    key_list = jax.random.split(jax.random.key(seed), 9)
    return {
        "residual": noise(key_list[0], (BLOCKS, SPEC, CELLS), 1.0, 6.0, ((0, 512),), jnp.float32),
        "kin_inverse": draw_kin_inverse(jax.random.fold_in(key_list[8], 71), 0),
        "cell_weight": jnp.clip(jnp.exp(math.log(1.0) - 0.6931472 * jax.random.uniform(key_list[2], (BLOCKS, CELLS), jnp.float32) ** block_levels(key_list[2], (BLOCKS, CELLS), ((0, 512),), -0.2, 0.2)), 0.5, 1.0),
        "upwind_frac": jnp.clip(0.2 + 0.5 * jax.random.uniform(key_list[3], (BLOCKS, UPW, CELLS), jnp.float32) ** block_levels(key_list[3], (BLOCKS, UPW, CELLS), ((0, 512),), -0.2, 0.2), 0.2, 0.7),
        "block_level": draw_block_level(jax.random.fold_in(key_list[8], 71), 0),
        "send_in": draw_send_in(jax.random.fold_in(key_list[8], 71), 0),
        "send_down": draw_send_down(jax.random.fold_in(key_list[8], 71), 0),
        "upwind_slot": draw_upwind_slot(jax.random.fold_in(key_list[8], 71), 0),
    }


def resolve(send_in, send_down, upwind_slot):
    rounds = LEVELS - 1
    block_ids = jnp.arange(BLOCKS, dtype=jnp.int32)[:, None]
    device_id = block_ids // BLK_DEV
    section_id = device_id // N_BLK
    owner_id = device_id % N_BLK
    base_in = BLK_DEV + 1
    base_down = base_in + rounds * N_BLK
    in_part = jnp.clip(upwind_slot - base_in, 0, rounds * N_BLK - 1).astype(jnp.int32)
    peer_dev = section_id * N_BLK + in_part % N_BLK
    peer_local = send_in.reshape(-1)[((peer_dev * rounds + in_part // N_BLK) * N_BLK + owner_id).astype(jnp.int32)]
    down_part = jnp.clip(upwind_slot - base_down, 0, rounds * N_BLK - 1).astype(jnp.int32)
    upper_dev = jnp.maximum(section_id - 1, 0) * N_BLK + down_part % N_BLK
    upper_local = send_down.reshape(-1)[((upper_dev * rounds + down_part // N_BLK) * N_BLK + owner_id).astype(jnp.int32)]
    local_ids = jnp.where(upwind_slot < BLK_DEV, device_id * BLK_DEV + upwind_slot, BLOCKS)
    peer_ids = jnp.where(peer_local < BLK_DEV, peer_dev * BLK_DEV + peer_local, BLOCKS)
    upper_ids = jnp.where((upper_local < BLK_DEV) & (section_id > 0), upper_dev * BLK_DEV + upper_local, BLOCKS)
    chosen = jnp.where(upwind_slot <= BLK_DEV, local_ids, jnp.where(upwind_slot < base_down, peer_ids, upper_ids))
    return chosen.astype(jnp.int32)


def reference(residual, kin_inverse, cell_weight, upwind_frac, block_level, send_in, send_down, upwind_slot):
    source_ids = resolve(send_in, send_down, upwind_slot)
    padding = jnp.zeros((1, SPEC, CELLS), jnp.float32)
    solution = jnp.concatenate([jnp.zeros((BLOCKS, SPEC, CELLS), jnp.float32), padding], axis=0)
    for level_id in range(LEVELS):
        inflow = residual
        for neighbour in range(UPW):
            inflow = inflow + upwind_frac[:, neighbour, None, :] * solution[source_ids[:, neighbour]]
        solved = cell_weight[:, None, :] * jnp.einsum("bij,bjc->bic", kin_inverse, inflow, precision=lax.Precision.HIGHEST)
        updated = jnp.where((block_level == level_id)[:, None, None], solved, solution[:BLOCKS])
        solution = jnp.concatenate([updated, padding], axis=0)
    return solution[:BLOCKS]
```

```python
import functools

import jax
import jax.numpy as jnp
from jax import lax
from jax.experimental import pallas as pl
from jax.experimental.pallas import tpu as pltpu
from jax.sharding import PartitionSpec as P

LEVELS = 6
ROUNDS = 5
CAP = 16
BLOCKS = 48
UPW = 4
PEERS = 32
ZERO = LEVELS * CAP
ARRIVED = ZERO + 1
STORE = ARRIVED + 2 * ROUNDS * PEERS
T_BLOCK, T_REF = 0, 96
T_SEND = T_REF + 96 * UPW
T_SLOT = T_SEND + 2 * ROUNDS * PEERS
T_LEN = T_SLOT + BLOCKS
MESH = pl.DeviceIdType.MESH


def solve_level(level, tab, residual, kin, weight, frac, store):
    def one(k, _):
        place = level * CAP + k
        b = tab[T_BLOCK + place]
        inflow = residual[b]
        fractions = frac[b]
        for j in range(UPW):
            source = store[tab[T_REF + place * UPW + j]]
            inflow = inflow + fractions[j : j + 1, :] * source
        mixed = jnp.dot(
            kin[b], inflow, precision=lax.Precision.HIGHEST, preferred_element_type=jnp.float32
        )
        store[place] = weight[b] * mixed
        return 0

    lax.fori_loop(0, CAP, one, 0, unroll=4)


def kernel(
    sections, tab, residual, kin, weight, frac, out, store, sendb, arrived, send_sem, recv_sem
):
    sec = lax.axis_index("section")
    me = lax.axis_index("blk")
    has_next = sec < sections - 1
    has_prev = sec > 0
    barrier = pltpu.get_barrier_semaphore()

    def greet(o, _):
        peer = lax.rem(me + o, PEERS)

        @pl.when(o > 0)
        def _():
            pl.semaphore_signal(
                barrier, inc=1, device_id={"section": sec, "blk": peer}, device_id_type=MESH
            )

        @pl.when(has_prev)
        def _():
            pl.semaphore_signal(
                barrier, inc=1, device_id={"section": sec - 1, "blk": peer}, device_id_type=MESH
            )

        return 0

    lax.fori_loop(0, PEERS, greet, 0)
    store[ZERO] = jnp.zeros(store.shape[1:], jnp.float32)
    solve_level(0, tab, residual, kin, weight, frac, store)

    @pl.when(has_next)
    def _():
        pl.semaphore_wait(barrier, 2 * PEERS - 1)

    @pl.when(jnp.logical_not(has_next))
    def _():
        pl.semaphore_wait(barrier, PEERS - 1)

    def copy_to(way, level, peer, section):
        return pltpu.make_async_remote_copy(
            src_ref=sendb.at[way, level, peer],
            dst_ref=arrived.at[way, level, me],
            send_sem=send_sem.at[way, level],
            recv_sem=recv_sem.at[way, level],
            device_id={"section": section, "blk": peer},
            device_id_type=MESH,
        )

    def one_round(level, _):
        def send(o, _):
            peer = lax.rem(me + o, PEERS)
            sendb[0, level, peer] = store[tab[T_SEND + level * PEERS + peer]]

            @pl.when(o > 0)
            def _():
                copy_to(0, level, peer, sec).start()

            @pl.when(has_next)
            def _():
                sendb[1, level, peer] = store[tab[T_SEND + (ROUNDS + level) * PEERS + peer]]
                copy_to(1, level, peer, sec + 1).start()

            return 0

        lax.fori_loop(0, PEERS, send, 0)

        some = arrived.at[0, level, pl.ds(0, PEERS - 1)]
        pltpu.make_async_copy(some, some, recv_sem.at[0, level]).wait()

        def keep_in(i, _):
            store[ARRIVED + level * PEERS + i] = arrived[0, level, i]
            return 0

        own = sendb[0, level, me]
        lax.fori_loop(0, PEERS, keep_in, 0, unroll=8)
        store[ARRIVED + level * PEERS + me] = own

        base = ARRIVED + (ROUNDS + level) * PEERS

        @pl.when(has_prev)
        def _():
            every = arrived.at[1, level]
            pltpu.make_async_copy(every, every, recv_sem.at[1, level]).wait()

            def keep_down(i, _):
                store[base + i] = arrived[1, level, i]
                return 0

            lax.fori_loop(0, PEERS, keep_down, 0, unroll=8)

        @pl.when(jnp.logical_not(has_prev))
        def _():
            def blank(i, _):
                store[base + i] = jnp.zeros(store.shape[1:], jnp.float32)
                return 0

            lax.fori_loop(0, PEERS, blank, 0, unroll=8)

        solve_level(level + 1, tab, residual, kin, weight, frac, store)
        return 0

    lax.fori_loop(0, ROUNDS, one_round, 0)

    def give(b, _):
        out[b] = store[tab[T_SLOT + b]]
        return 0

    lax.fori_loop(0, BLOCKS, give, 0, unroll=8)

    def finish(level, _):
        some = sendb.at[0, level, pl.ds(0, PEERS - 1)]
        pltpu.make_async_copy(some, some, send_sem.at[0, level]).wait()

        @pl.when(has_next)
        def _():
            every = sendb.at[1, level]
            pltpu.make_async_copy(every, every, send_sem.at[1, level]).wait()

        return 0

    lax.fori_loop(0, ROUNDS, finish, 0)


def tables(block_level, send_in, send_down, upwind_slot):
    ids = jnp.arange(BLOCKS, dtype=jnp.int32)
    places = jnp.arange(LEVELS * CAP, dtype=jnp.int32)
    same = (block_level[:, None] == block_level[None, :]) & (ids[None, :] < ids[:, None])
    slot = block_level * CAP + jnp.sum(same.astype(jnp.int32), axis=1)

    def slot_of(local):
        hit = local[..., None] == ids
        return ZERO + jnp.sum(jnp.where(hit, slot - ZERO, 0), axis=-1)

    sends = slot_of(jnp.concatenate([send_in.reshape(-1), send_down.reshape(-1)]))
    refs = jnp.where(
        upwind_slot <= BLOCKS, slot_of(upwind_slot), upwind_slot - (BLOCKS + 1) + ARRIVED
    )
    at = slot[None, :] == places[:, None]
    block_at = jnp.sum(jnp.where(at, ids, 0), axis=1)
    refs_at = ZERO + jnp.sum(jnp.where(at[:, :, None], refs[None] - ZERO, 0), axis=1)
    return jnp.concatenate([block_at, refs_at.reshape(-1), sends, slot])


def shards(
    residual, kin_inverse, cell_weight, upwind_frac, block_level, send_in, send_down, upwind_slot
):
    blocks, species, cells = residual.shape
    tab = tables(block_level, send_in, send_down, upwind_slot)
    vmem = pl.BlockSpec(memory_space=pltpu.VMEM)
    return pl.pallas_call(
        functools.partial(kernel, lax.axis_size("section")),
        out_shape=jax.ShapeDtypeStruct(residual.shape, jnp.float32),
        in_specs=[pl.BlockSpec(memory_space=pltpu.SMEM)] + [vmem] * 4,
        out_specs=vmem,
        scratch_shapes=[
            pltpu.VMEM((STORE, species, cells), jnp.float32),
            pltpu.VMEM((2, ROUNDS, PEERS, species, cells), jnp.float32),
            pltpu.VMEM((2, ROUNDS, PEERS, species, cells), jnp.float32),
            pltpu.SemaphoreType.DMA((2, ROUNDS)),
            pltpu.SemaphoreType.DMA((2, ROUNDS)),
        ],
        compiler_params=pltpu.CompilerParams(
            collective_id=0, has_side_effects=True, vmem_limit_bytes=40 * 1024 * 1024
        ),
    )(tab, residual, kin_inverse, cell_weight[:, None, :], upwind_frac)


def solution(mesh):
    both = ("section", "blk")
    return jax.shard_map(
        shards,
        mesh=mesh,
        in_specs=(
            P(both, None, None),
            P(both, None, None),
            P(both, None),
            P(both, None, None),
            P(both),
            P(both, None, None),
            P(both, None, None),
            P(both, None),
        ),
        out_specs=P(both, None, None),
        check_vma=False,
    )
```

```python
import functools

import jax
import jax.numpy as jnp
from jax import lax
from jax.experimental import pallas as pl
from jax.experimental.pallas import tpu as pltpu
from jax.sharding import PartitionSpec as P

LEVELS = 6
ROUNDS = 5
CAP = 16
BLOCKS = 48
GROUP = 8
UPW = 4
ZS, XS = 8, 4
PEERS = XS * ZS
NEAR = 5
ZERO = LEVELS * CAP
ARRIVED = ZERO + 1
STORE = ARRIVED + 2 * ROUNDS * PEERS
T_BLOCK, T_REF, T_SLOT, T_SEND, T_ROWS = 0, 1, 5, 8, 24
E_ROW1 = 2 * XS * NEAR
E_ROW2 = E_ROW1 + 4 * XS
ENTRIES = E_ROW2 + 2 * XS
MESH = pl.DeviceIdType.MESH
ROWS = 16
HALF = 64


def swap(value):
    return pltpu.roll(value, HALF, 1)


def low_lanes(rows):
    return lax.broadcasted_iota(jnp.int32, (rows, 2 * HALF), 1) < HALF


def fold(half, top, bottom):
    low = low_lanes(top.shape[0])
    return (
        jnp.where(low, top, swap(bottom)) if half == 0 else jnp.where(low, swap(top), bottom)
    )


def make_table(z, level_ref, upwind_ref, send_in_ref, send_down_ref, table):
    square = (BLOCKS, BLOCKS)
    wide = (BLOCKS, 2 * HALF)
    row, col = (lax.broadcasted_iota(jnp.int32, square, d) for d in range(2))

    def down(mask, value):
        return jnp.sum(jnp.where(mask, value, 0), axis=0, keepdims=True)

    def upright(value):
        return jnp.sum(
            jnp.where(row == col, jnp.broadcast_to(value, square), 0), axis=1, keepdims=True
        )

    level = level_ref[...]
    level_col = upright(level)
    same = jnp.broadcast_to(level, square) == level_col
    rank_col = jnp.sum(jnp.where(same & (col < row), 1, 0), axis=1, keepdims=True)
    slot_col = level_col * CAP + rank_col
    table[...] = jnp.zeros(table.shape, jnp.int32)
    table[T_SLOT : T_SLOT + 1, :BLOCKS] = down(row == col, slot_col)
    here = slot_col == lax.broadcasted_iota(jnp.int32, wide, 1)
    table[T_BLOCK : T_BLOCK + 1, :] = down(here, lax.broadcasted_iota(jnp.int32, wide, 0))
    for j in range(UPW):
        t = upwind_ref[j : j + 1, :]
        local = ZERO + down(t == row, slot_col - ZERO)
        number = jnp.maximum(t - (BLOCKS + 1), 0)
        owner_z = number & (ZS - 1)
        remote = ARRIVED + number - owner_z + ((owner_z - z + (2 + ZS)) & (ZS - 1))
        ref = jnp.where(t <= BLOCKS, local, remote)
        table[T_REF + j : T_REF + j + 1, :] = ZERO + down(here, upright(ref) - ZERO)
    local_id = lax.broadcasted_iota(jnp.int32, (BLOCKS, PEERS), 0)
    for way, sent in enumerate((send_in_ref, send_down_ref)):
        for r in range(ROUNDS):
            place = T_SEND + way * ROUNDS + r
            table[place : place + 1, :PEERS] = CAP + down(sent[r] == local_id, rank_col - CAP)


def kernel(
    sections,
    level_ref,
    upwind_ref,
    send_in_ref,
    send_down_ref,
    residual,
    kin,
    weight,
    frac,
    out,
    table,
    around,
    tab,
    tabs,
    store,
    near,
    packs,
    arrived,
    sendb,
    pack_send,
    pack_recv,
    uni_send,
    uni_recv,
    tab_send,
    tab_recv,
    tab_local,
):
    sec = lax.axis_index("section")
    me = lax.axis_index("blk")
    x, z = me // ZS, lax.rem(me, ZS)
    has_next = sec < sections - 1
    has_prev = sec > 0
    barrier = pltpu.get_barrier_semaphore()
    zeros = jnp.zeros((ROWS, 2 * HALF), jnp.float32)

    def at(section, xo, zo):
        peer = lax.rem(x + xo, XS) * ZS + lax.rem(z + zo + ZS, ZS)
        return {"section": section, "blk": peer}

    def greet(xo, _):
        for zo in range(-2, 3):
            if zo == 0:

                @pl.when(xo > 0)
                def _():
                    pl.semaphore_signal(
                        barrier, inc=1, device_id=at(sec, xo, 0), device_id_type=MESH
                    )
            else:
                pl.semaphore_signal(
                    barrier, inc=1, device_id=at(sec, xo, zo), device_id_type=MESH
                )

            @pl.when(has_prev)
            def _(zo=zo):
                pl.semaphore_signal(
                    barrier, inc=1, device_id=at(sec - 1, xo, zo), device_id_type=MESH
                )

        return 0

    lax.fori_loop(0, XS, greet, 0)

    def solve(half, level, last=False):
        low = low_lanes(ROWS)

        def gather(k):
            place = level * CAP + k
            b = tab[T_BLOCK, place]
            whole = residual[b]
            inflow = fold(half, whole[:ROWS], whole[ROWS:])
            fractions = fold(half, frac[b], frac[b])
            for j in range(UPW):
                source = store[half, tab[T_REF + j, place]]
                inflow = inflow + fractions[j : j + 1, :] * source
            other = swap(inflow)
            both = jnp.concatenate(
                [jnp.where(low, inflow, other), jnp.where(low, other, inflow)], axis=0
            )
            coarse = both.astype(jnp.bfloat16)
            rest = (both - coarse.astype(jnp.float32)).astype(jnp.bfloat16)
            return b, jnp.concatenate([coarse, coarse, rest], axis=0)

        def group(g, _):
            spots = [g * GROUP + i for i in range(GROUP)]
            gathered = [gather(k) for k in spots]
            mixed = [
                jnp.dot(kin[b], terms, preferred_element_type=jnp.float32)
                for b, terms in gathered
            ]
            solved = [
                fold(half, weight[b], weight[b]) * jnp.where(low, m[:ROWS], m[ROWS:])
                for (b, _), m in zip(gathered, mixed)
            ]
            for k, value in zip(spots, solved):
                store[half, level * CAP + k] = value
                if not last:
                    packs[half, level, 2 * CAP + k] = value
            return 0

        lax.fori_loop(0, CAP // GROUP, group, 0)

    def pack_copy(half, level, source, target, zo):
        return pltpu.make_async_remote_copy(
            src_ref=packs.at[half, level, pl.ds(source * CAP, CAP)],
            dst_ref=packs.at[half, level, pl.ds(target * CAP, CAP)],
            send_sem=pack_send.at[half, level],
            recv_sem=pack_recv.at[half, level, target],
            device_id=at(sec, 0, zo),
            device_id_type=MESH,
        )

    def pack_wait(half, level, place):
        some = packs.at[half, level, pl.ds(place * CAP, CAP)]
        pltpu.make_async_copy(some, some, pack_recv.at[half, level, place]).wait()

    def send_own(half, level):
        pack_copy(half, level, 2, 1, 1).start()
        pack_copy(half, level, 2, 3, -1).start()

    def forward(half, level):
        pack_wait(half, level, 1)
        pack_copy(half, level, 1, 0, 1).start()
        pack_wait(half, level, 3)
        pack_copy(half, level, 3, 4, -1).start()

    def deliver(half, level):
        pack_wait(half, level, 0)
        pack_wait(half, level, 4)
        for p in range(NEAR):
            for k in range(CAP):
                near[p * (CAP + 1) + k] = packs[half, level, p * CAP + k]

        def to_column(xo, _):
            column = lax.rem(x + xo, XS) * ZS

            def fill(entry, way, p, zo):
                target = column + lax.rem(z + zo + ZS, ZS)
                chosen = tabs[p, way * ROUNDS + level, target]
                sendb[half, level, entry] = near[p * (CAP + 1) + chosen]

            def copy(entry, count, way, place, zo):
                return pltpu.make_async_remote_copy(
                    src_ref=sendb.at[half, level, pl.ds(entry, count)],
                    dst_ref=arrived.at[way, half, level, pl.ds(x * ZS + place, count)],
                    send_sem=uni_send.at[way, half, level],
                    recv_sem=uni_recv.at[way, half, level],
                    device_id=at(sec + way, xo, zo),
                    device_id_type=MESH,
                )

            def send_way(way):
                far = E_ROW2 + way * XS + xo
                if way == 0:
                    fill(far, way, 0, 2)
                    copy(far, 1, way, 6, 2).start()
                else:
                    fill(far, way, 4, -2)
                    copy(far, 1, way, 6, -2).start()
                up = E_ROW1 + way * XS + xo
                fill(up, way, 0, 1)
                copy(up, 1, way, 7, 1).start()
                down = E_ROW1 + (2 + way) * XS + xo
                fill(down, way, 4, -1)
                copy(down, 1, way, 5, -1).start()
                first = (way * XS + xo) * NEAR
                for p in range(NEAR):
                    fill(first + p, way, p, 0)
                if way == 0:

                    @pl.when(xo > 0)
                    def _():
                        copy(first, NEAR, way, 0, 0).start()
                else:
                    copy(first, NEAR, way, 0, 0).start()

            send_way(0)

            @pl.when(has_next)
            def _():
                send_way(1)

            return 0

        lax.fori_loop(0, XS, to_column, 0)

    def absorb(half, level):
        some = arrived.at[0, half, level, pl.ds(0, PEERS - NEAR)]
        pltpu.make_async_copy(some, some, uni_recv.at[0, half, level]).wait()
        base = ARRIVED + level * PEERS
        for i in range(PEERS):
            store[half, base + i] = arrived[0, half, level, i]
        for p in range(NEAR):
            store[half, base + x * ZS + p] = sendb[half, level, p]

        @pl.when(has_prev)
        def _():
            every = arrived.at[1, half, level]
            pltpu.make_async_copy(every, every, uni_recv.at[1, half, level]).wait()
            for i in range(PEERS):
                store[half, base + ROUNDS * PEERS + i] = arrived[1, half, level, i]

    for half in range(2):
        store[half, ZERO] = zeros
    for p in range(NEAR):
        near[p * (CAP + 1) + CAP] = zeros

    @pl.when(jnp.logical_not(has_prev))
    def _():
        def blank(i, _):
            for half in range(2):
                store[half, ARRIVED + ROUNDS * PEERS + i] = zeros
            return 0

        lax.fori_loop(0, ROUNDS * PEERS, blank, 0)

    make_table(z, level_ref, upwind_ref, send_in_ref, send_down_ref, table)
    own = pltpu.make_async_copy(table, tab, tab_local.at[NEAR])
    own.start()
    own.wait()
    solve(0, 0)

    @pl.when(has_next)
    def _():
        pl.semaphore_wait(barrier, 2 * XS * NEAR - 1)

    @pl.when(jnp.logical_not(has_next))
    def _():
        pl.semaphore_wait(barrier, XS * NEAR - 1)

    send_own(0, 0)
    for o in (-2, -1, 1, 2):
        pltpu.make_async_remote_copy(
            src_ref=table.at[pl.ds(T_SEND, 16)],
            dst_ref=around.at[2 - o],
            send_sem=tab_send,
            recv_sem=tab_recv.at[2 - o],
            device_id=at(sec, 0, o),
            device_id_type=MESH,
        ).start()
    solve(1, 0)
    send_own(1, 0)
    moves = []
    for p in range(NEAR):
        if p == 2:
            source = table.at[pl.ds(T_SEND, 16)]
        else:
            source = around.at[p]
            pltpu.make_async_copy(source, source, tab_recv.at[p]).wait()
        moves.append(pltpu.make_async_copy(source, tabs.at[p], tab_local.at[p]))
        moves[-1].start()
    for move in moves:
        move.wait()

    def one_round(level, _):
        forward(0, level)

        @pl.when(level > 0)
        def _():
            absorb(1, level - 1)
            solve(1, level)
            send_own(1, level)

        deliver(0, level)
        forward(1, level)
        absorb(0, level)

        @pl.when(level < ROUNDS - 1)
        def _():
            solve(0, level + 1)
            send_own(0, level + 1)

        deliver(1, level)
        return 0

    lax.fori_loop(0, ROUNDS, one_round, 0)
    solve(0, ROUNDS, last=True)
    absorb(1, ROUNDS - 1)
    solve(1, ROUNDS, last=True)

    def give(b, _):
        slot = tab[T_SLOT, b]
        first, second = store[0, slot], store[1, slot]
        low = low_lanes(ROWS)
        out[b, :ROWS] = jnp.where(low, first, swap(second))
        out[b, ROWS:] = jnp.where(low, swap(first), second)
        return 0

    lax.fori_loop(0, BLOCKS, give, 0, unroll=4)

    def finish(level, _):
        for half in range(2):
            some = packs.at[half, level, pl.ds(0, 4 * CAP)]
            pltpu.make_async_copy(some, some, pack_send.at[half, level]).wait()
            some = sendb.at[half, level, pl.ds(0, PEERS - NEAR)]
            pltpu.make_async_copy(some, some, uni_send.at[0, half, level]).wait()

            @pl.when(has_next)
            def _(half=half):
                some = sendb.at[half, level, pl.ds(0, PEERS)]
                pltpu.make_async_copy(some, some, uni_send.at[1, half, level]).wait()

        return 0

    lax.fori_loop(0, ROUNDS, finish, 0)
    some = around.at[pl.ds(0, NEAR - 1)]
    pltpu.make_async_copy(some, some, tab_send).wait()


def shards(
    residual, kin_inverse, cell_weight, upwind_frac, block_level, send_in, send_down, upwind_slot
):
    blocks, species, cells = residual.shape
    coarse = lax.reduce_precision(kin_inverse, 8, 7)
    rest = (kin_inverse - coarse).astype(jnp.bfloat16)
    coarse = coarse.astype(jnp.bfloat16)
    kin = jnp.concatenate([coarse, rest, coarse], axis=2)
    vmem = pl.BlockSpec(memory_space=pltpu.VMEM)
    half = (ROWS, 2 * HALF)
    return pl.pallas_call(
        functools.partial(kernel, lax.axis_size("section")),
        out_shape=jax.ShapeDtypeStruct(residual.shape, jnp.float32),
        in_specs=[vmem] * 8,
        out_specs=vmem,
        scratch_shapes=[
            pltpu.VMEM((T_ROWS, 2 * HALF), jnp.int32),
            pltpu.VMEM((NEAR, 16, 2 * HALF), jnp.int32),
            pltpu.SMEM((T_ROWS, 2 * HALF), jnp.int32),
            pltpu.SMEM((NEAR, 16, 2 * HALF), jnp.int32),
            pltpu.VMEM((2, STORE, *half), jnp.float32),
            pltpu.VMEM((NEAR * (CAP + 1), *half), jnp.float32),
            pltpu.VMEM((2, ROUNDS, NEAR * CAP, *half), jnp.float32),
            pltpu.VMEM((2, 2, ROUNDS, PEERS, *half), jnp.float32),
            pltpu.VMEM((2, ROUNDS, ENTRIES, *half), jnp.float32),
            pltpu.SemaphoreType.DMA((2, ROUNDS)),
            pltpu.SemaphoreType.DMA((2, ROUNDS, NEAR)),
            pltpu.SemaphoreType.DMA((2, 2, ROUNDS)),
            pltpu.SemaphoreType.DMA((2, 2, ROUNDS)),
            pltpu.SemaphoreType.DMA,
            pltpu.SemaphoreType.DMA((NEAR,)),
            pltpu.SemaphoreType.DMA((NEAR + 1,)),
        ],
        compiler_params=pltpu.CompilerParams(
            collective_id=0, has_side_effects=True, vmem_limit_bytes=44 * 1024 * 1024
        ),
    )(
        block_level[None],
        upwind_slot.T,
        send_in.transpose(1, 0, 2),
        send_down.transpose(1, 0, 2),
        residual,
        kin,
        cell_weight[:, None, :],
        upwind_frac,
    )


def solution(mesh):
    both = ("section", "blk")
    return jax.shard_map(
        shards,
        mesh=mesh,
        in_specs=(
            P(both, None, None),
            P(both, None, None),
            P(both, None),
            P(both, None, None),
            P(both),
            P(both, None, None),
            P(both, None, None),
            P(both, None),
        ),
        out_specs=P(both, None, None),
        check_vma=False,
    )
```

```python
import functools

import jax
import jax.numpy as jnp
from jax import lax
from jax.experimental import pallas as pl
from jax.experimental.pallas import tpu as pltpu
from jax.sharding import PartitionSpec as P

LEVELS = 6
ROUNDS = 5
CAP = 16
BLOCKS = 48
GROUP = 8
UPW = 4
ZS, XS = 8, 4
PEERS = XS * ZS
OFFSETS = (0, -1, 1, -2, 2)
NEAR = len(OFFSETS)
ORDER = (2, 1, 3, 0)
ZERO = LEVELS * CAP
ARRIVED = ZERO + 1
STORE = ARRIVED + 2 * ROUNDS * PEERS
T_BLOCK, T_REF, T_SLOT, T_SEND, T_ROWS = 0, 1, 5, 8, 24
E_ROW1 = 2 * XS * NEAR
E_ROW2 = E_ROW1 + 4 * XS
ENTRIES = E_ROW2 + 2 * XS
MESH = pl.DeviceIdType.MESH
ROWS = 8
LANES = 128
PARTS = 4
WIDTH = LANES // PARTS
SLOTS = ROUNDS * PARTS


def groups_of(rows):
    return lax.broadcasted_iota(jnp.int32, (rows, LANES), 1) // WIDTH


def pick(group, values):
    result = values[PARTS - 1]
    for g in range(PARTS - 2, -1, -1):
        result = jnp.where(group == g, values[g], result)
    return result


def turns(value):
    return [value] + [pltpu.roll(value, WIDTH * t, 1) for t in range(1, PARTS)]


def make_table(z, level_ref, upwind_ref, send_in_ref, send_down_ref, table):
    square = (BLOCKS, BLOCKS)
    wide = (BLOCKS, LANES)
    row, col = (lax.broadcasted_iota(jnp.int32, square, d) for d in range(2))

    def down(mask, value):
        return jnp.sum(jnp.where(mask, value, 0), axis=0, keepdims=True)

    def upright(value):
        return jnp.sum(
            jnp.where(row == col, jnp.broadcast_to(value, square), 0), axis=1, keepdims=True
        )

    level = level_ref[...]
    level_col = upright(level)
    same = jnp.broadcast_to(level, square) == level_col
    rank_col = jnp.sum(jnp.where(same & (col < row), 1, 0), axis=1, keepdims=True)
    slot_col = level_col * CAP + rank_col
    table[...] = jnp.zeros(table.shape, jnp.int32)
    table[T_SLOT : T_SLOT + 1, :BLOCKS] = down(row == col, slot_col)
    here = slot_col == lax.broadcasted_iota(jnp.int32, wide, 1)
    table[T_BLOCK : T_BLOCK + 1, :] = down(here, lax.broadcasted_iota(jnp.int32, wide, 0))
    for j in range(UPW):
        t = upwind_ref[j : j + 1, :]
        local = ZERO + down(t == row, slot_col - ZERO)
        number = jnp.maximum(t - (BLOCKS + 1), 0)
        owner_z = number & (ZS - 1)
        away = (owner_z - z + ZS) & (ZS - 1)
        spot = jnp.zeros_like(away)
        for place, o in enumerate(OFFSETS + (3, 4, -3)):
            spot = jnp.where(away == o % ZS, place, spot)
        remote = ARRIVED + number - owner_z + spot
        ref = jnp.where(t <= BLOCKS, local, remote)
        table[T_REF + j : T_REF + j + 1, :] = ZERO + down(here, upright(ref) - ZERO)
    local_id = lax.broadcasted_iota(jnp.int32, (BLOCKS, PEERS), 0)
    for way, sent in enumerate((send_in_ref, send_down_ref)):
        for r in range(ROUNDS):
            place = T_SEND + way * ROUNDS + r
            table[place : place + 1, :PEERS] = CAP + down(sent[r] == local_id, rank_col - CAP)


def kernel(
    sections,
    level_ref,
    upwind_ref,
    send_in_ref,
    send_down_ref,
    residual,
    kin_ref,
    weight,
    frac,
    out,
    table,
    around,
    tab,
    tabs,
    kin,
    rights,
    factors,
    store,
    near,
    packs,
    arrived,
    sendb,
    pack_send,
    pack_recv,
    uni_send,
    uni_recv,
    tab_send,
    tab_recv,
    tab_local,
):
    sec = lax.axis_index("section")
    me = lax.axis_index("blk")
    x, z = me // ZS, lax.rem(me, ZS)
    has_next = sec < sections - 1
    has_prev = sec > 0
    columns = [lax.rem(x + xo, XS) * ZS for xo in range(XS)]
    rows = {zo: lax.rem(z + zo + ZS, ZS) for zo in range(-2, 3)}
    barrier = pltpu.get_barrier_semaphore()
    zeros = jnp.zeros((ROWS, LANES), jnp.float32)

    def at(section, xo, zo):
        return {"section": section, "blk": columns[xo] + rows[zo]}

    for xo in range(XS):
        for zo in range(-2, 3):
            if xo or zo:
                pl.semaphore_signal(
                    barrier, inc=1, device_id=at(sec, xo, zo), device_id_type=MESH
                )

    @pl.when(has_prev)
    def _():
        for xo in range(XS):
            for zo in range(-2, 3):
                pl.semaphore_signal(
                    barrier, inc=1, device_id=at(sec - 1, xo, zo), device_id_type=MESH
                )

    group = groups_of(ROWS)

    def prepare(b, _):
        exact = kin_ref[b]
        coarse = exact.astype(jnp.bfloat16).astype(jnp.float32)
        kin[b] = jnp.concatenate([coarse, exact - coarse, coarse], axis=1).astype(jnp.bfloat16)
        whole = residual[b]
        turned = [turns(whole[g * ROWS : (g + 1) * ROWS]) for g in range(PARTS)]
        scales = turns(jnp.concatenate([frac[b], weight[b], weight[b], frac[b][:2]], axis=0))
        for part in range(PARTS):
            rights[part, b] = pick(
                group, [turned[g][(g - part) % PARTS] for g in range(PARTS)]
            )
            factors[part, b] = pick(
                group, [scales[(g - part) % PARTS] for g in range(PARTS)]
            )
        return 0

    def solve(part, level, slot, last=False):
        def gather(k):
            place = level * CAP + k
            b = tab[T_BLOCK, place]
            inflow = rights[part, b]
            factor = factors[part, b]
            for j in range(UPW):
                source = store[part, tab[T_REF + j, place]]
                inflow = inflow + factor[j : j + 1, :] * source
            turned = turns(inflow)
            all_species = jnp.concatenate(
                [
                    pick(group, [turned[(to - g) % PARTS] for to in range(PARTS)])
                    for g in range(PARTS)
                ],
                axis=0,
            )
            coarse = all_species.astype(jnp.bfloat16)
            rest = (all_species - coarse.astype(jnp.float32)).astype(jnp.bfloat16)
            return b, factor[UPW : UPW + 1, :], jnp.concatenate([coarse, coarse, rest], axis=0)

        def batch(i, _):
            spots = [i * GROUP + k for k in range(GROUP)]
            gathered = [gather(k) for k in spots]
            mixed = [
                jnp.dot(kin[b], terms, preferred_element_type=jnp.float32)
                for b, _, terms in gathered
            ]
            solved = [
                scale * pick(group, [m[g * ROWS : (g + 1) * ROWS] for g in range(PARTS)])
                for (_, scale, _), m in zip(gathered, mixed)
            ]
            for k, value in zip(spots, solved):
                store[part, level * CAP + k] = value
                if not last:
                    packs[slot, k] = value
                    near[part, k] = value
            return 0

        lax.fori_loop(0, CAP // GROUP, batch, 0)

    def pack_copy(slot, source, target, zo):
        return pltpu.make_async_remote_copy(
            src_ref=packs.at[slot, pl.ds(source * CAP, CAP)],
            dst_ref=packs.at[slot, pl.ds(target * CAP, CAP)],
            send_sem=pack_send.at[slot],
            recv_sem=pack_recv.at[slot, target],
            device_id=at(sec, 0, zo),
            device_id_type=MESH,
        )

    def pack_wait(slot, p):
        some = packs.at[slot, pl.ds(p * CAP, CAP)]
        pltpu.make_async_copy(some, some, pack_recv.at[slot, p]).wait()

    def hold(slot, p):
        part = lax.rem(slot, PARTS)
        for k in range(CAP):
            near[part, p * (CAP + 1) + k] = packs[slot, p * CAP + k]

    def fill(slot, entry, way, p, xo, zo):
        level, part = slot // PARTS, lax.rem(slot, PARTS)
        chosen = tabs[p, way * ROUNDS + level, columns[xo] + rows[zo]]
        sendb[slot, entry] = near[part, p * (CAP + 1) + chosen]

    def copy(slot, entry, count, way, place, xo, zo):
        return pltpu.make_async_remote_copy(
            src_ref=sendb.at[slot, pl.ds(entry, count)],
            dst_ref=arrived.at[way, slot, pl.ds(x * ZS + place, count)],
            send_sem=uni_send.at[way, slot],
            recv_sem=uni_recv.at[way, slot],
            device_id=at(sec + way, xo, zo),
            device_id_type=MESH,
        )

    def to_row(slot, way, xo, first, count):
        entry = (way * XS + xo) * NEAR
        for p in range(first, first + count):
            fill(slot, entry + p, way, p, xo, 0)
        if way or xo:
            copy(slot, entry + first, count, way, first, xo, 0).start()

    def to_columns(send_way):
        for xo in ORDER:
            send_way(xo, 0)

        @pl.when(has_next)
        def _():
            for xo in ORDER:
                send_way(xo, 1)

    def send_own(slot):
        pack_copy(slot, 0, 1, 1).start()
        pack_copy(slot, 0, 2, -1).start()

    def forward(slot):
        pack_wait(slot, 1)
        pack_copy(slot, 1, 3, 1).start()
        pack_wait(slot, 2)
        pack_copy(slot, 2, 4, -1).start()
        hold(slot, 1)
        hold(slot, 2)
        to_columns(lambda xo, way: to_row(slot, way, xo, 0, 3))

    def deliver(slot):
        for p in (3, 4):
            pack_wait(slot, p)
            hold(slot, p)

        def send_way(xo, way):
            far = E_ROW2 + way * XS + xo
            p, zo = ((3, 2), (4, -2))[way]
            fill(slot, far, way, p, xo, zo)
            copy(slot, far, 1, way, 6, xo, zo).start()
            up = E_ROW1 + way * XS + xo
            fill(slot, up, way, 3, xo, 1)
            copy(slot, up, 1, way, 7, xo, 1).start()
            down = E_ROW1 + (2 + way) * XS + xo
            fill(slot, down, way, 4, xo, -1)
            copy(slot, down, 1, way, 5, xo, -1).start()
            to_row(slot, way, xo, 3, 2)

        to_columns(send_way)

    def absorb(slot):
        level, part = slot // PARTS, lax.rem(slot, PARTS)
        some = arrived.at[0, slot, pl.ds(0, PEERS - NEAR)]
        pltpu.make_async_copy(some, some, uni_recv.at[0, slot]).wait()
        base = ARRIVED + level * PEERS
        for i in range(PEERS):
            store[part, base + i] = arrived[0, slot, i]
        for p in range(NEAR):
            store[part, base + x * ZS + p] = sendb[slot, p]

        @pl.when(has_prev)
        def _():
            every = arrived.at[1, slot]
            pltpu.make_async_copy(every, every, uni_recv.at[1, slot]).wait()
            for i in range(PEERS):
                store[part, base + ROUNDS * PEERS + i] = arrived[1, slot, i]

    make_table(z, level_ref, upwind_ref, send_in_ref, send_down_ref, table)
    moves = [
        pltpu.make_async_copy(table, tab, tab_local.at[NEAR]),
        pltpu.make_async_copy(table.at[pl.ds(T_SEND, 16)], tabs.at[0], tab_local.at[0]),
    ]
    for move in moves:
        move.start()
    lax.fori_loop(0, BLOCKS, prepare, 0, unroll=8)
    for part in range(PARTS):
        store[part, ZERO] = zeros
        for p in range(NEAR):
            near[part, p * (CAP + 1) + CAP] = zeros

    @pl.when(jnp.logical_not(has_prev))
    def _():
        def blank(i, _):
            for part in range(PARTS):
                store[part, ARRIVED + ROUNDS * PEERS + i] = zeros
            return 0

        lax.fori_loop(0, ROUNDS * PEERS, blank, 0)

    for move in moves:
        move.wait()
    solve(0, 0, 0)

    @pl.when(has_next)
    def _():
        pl.semaphore_wait(barrier, 2 * XS * NEAR - 1)

    @pl.when(jnp.logical_not(has_next))
    def _():
        pl.semaphore_wait(barrier, XS * NEAR - 1)

    send_own(0)
    for o in OFFSETS[1:]:
        p = OFFSETS.index(-o)
        pltpu.make_async_remote_copy(
            src_ref=table.at[pl.ds(T_SEND, 16)],
            dst_ref=around.at[p],
            send_sem=tab_send,
            recv_sem=tab_recv.at[p],
            device_id=at(sec, 0, o),
            device_id_type=MESH,
        ).start()

    def first(part, _):
        solve(part, 0, part)
        send_own(part)
        return 0

    lax.fori_loop(1, PARTS, first, 0)
    moves = []
    for p in range(1, NEAR):
        source = around.at[p]
        pltpu.make_async_copy(source, source, tab_recv.at[p]).wait()
        moves.append(pltpu.make_async_copy(source, tabs.at[p], tab_local.at[p]))
        moves[-1].start()
    for move in moves:
        move.wait()
    forward(0)

    def step(slot, _):
        @pl.when(slot >= PARTS)
        def _():
            absorb(slot - PARTS)
            solve(lax.rem(slot, PARTS), slot // PARTS, slot)
            send_own(slot)

        forward(slot - 1)
        deliver(slot - 2)
        return 0

    lax.fori_loop(2, SLOTS, step, 0)
    absorb(SLOTS - PARTS)
    solve(0, ROUNDS, 0, last=True)
    forward(SLOTS - 1)
    deliver(SLOTS - 2)
    absorb(SLOTS - PARTS + 1)
    solve(1, ROUNDS, 0, last=True)
    deliver(SLOTS - 1)

    def tail(part, _):
        absorb(SLOTS - PARTS + part)
        solve(part, ROUNDS, 0, last=True)
        return 0

    lax.fori_loop(2, PARTS, tail, 0)

    def give(b, _):
        place = tab[T_SLOT, b]
        turned = [turns(store[part, place]) for part in range(PARTS)]
        for g in range(PARTS):
            out[b, g * ROWS : (g + 1) * ROWS] = pick(
                group, [turned[part][(part - g) % PARTS] for part in range(PARTS)]
            )
        return 0

    lax.fori_loop(0, BLOCKS, give, 0, unroll=4)

    def finish(slot, _):
        some = packs.at[slot, pl.ds(0, 4 * CAP)]
        pltpu.make_async_copy(some, some, pack_send.at[slot]).wait()
        some = sendb.at[slot, pl.ds(0, PEERS - NEAR)]
        pltpu.make_async_copy(some, some, uni_send.at[0, slot]).wait()

        @pl.when(has_next)
        def _():
            some = sendb.at[slot, pl.ds(0, PEERS)]
            pltpu.make_async_copy(some, some, uni_send.at[1, slot]).wait()

        return 0

    lax.fori_loop(0, SLOTS, finish, 0)
    some = around.at[pl.ds(0, NEAR - 1)]
    pltpu.make_async_copy(some, some, tab_send).wait()


def shards(
    residual, kin_inverse, cell_weight, upwind_frac, block_level, send_in, send_down, upwind_slot
):
    blocks, species, cells = residual.shape
    vmem = pl.BlockSpec(memory_space=pltpu.VMEM)
    piece = (ROWS, LANES)
    return pl.pallas_call(
        functools.partial(kernel, lax.axis_size("section")),
        out_shape=jax.ShapeDtypeStruct(residual.shape, jnp.float32),
        in_specs=[vmem] * 8,
        out_specs=vmem,
        scratch_shapes=[
            pltpu.VMEM((T_ROWS, LANES), jnp.int32),
            pltpu.VMEM((NEAR, 16, LANES), jnp.int32),
            pltpu.SMEM((T_ROWS, LANES), jnp.int32),
            pltpu.SMEM((NEAR, 16, LANES), jnp.int32),
            pltpu.VMEM((blocks, species, 3 * species), jnp.bfloat16),
            pltpu.VMEM((PARTS, BLOCKS, *piece), jnp.float32),
            pltpu.VMEM((PARTS, BLOCKS, *piece), jnp.float32),
            pltpu.VMEM((PARTS, STORE, *piece), jnp.float32),
            pltpu.VMEM((PARTS, NEAR * (CAP + 1), *piece), jnp.float32),
            pltpu.VMEM((SLOTS, NEAR * CAP, *piece), jnp.float32),
            pltpu.VMEM((2, SLOTS, PEERS, *piece), jnp.float32),
            pltpu.VMEM((SLOTS, ENTRIES, *piece), jnp.float32),
            pltpu.SemaphoreType.DMA((SLOTS,)),
            pltpu.SemaphoreType.DMA((SLOTS, NEAR)),
            pltpu.SemaphoreType.DMA((2, SLOTS)),
            pltpu.SemaphoreType.DMA((2, SLOTS)),
            pltpu.SemaphoreType.DMA,
            pltpu.SemaphoreType.DMA((NEAR,)),
            pltpu.SemaphoreType.DMA((NEAR + 1,)),
        ],
        compiler_params=pltpu.CompilerParams(
            collective_id=0, has_side_effects=True, vmem_limit_bytes=44 * 1024 * 1024
        ),
    )(
        block_level[None],
        upwind_slot.T,
        send_in.transpose(1, 0, 2),
        send_down.transpose(1, 0, 2),
        residual,
        kin_inverse,
        cell_weight[:, None, :],
        upwind_frac,
    )


def solution(mesh):
    both = ("section", "blk")
    return jax.shard_map(
        shards,
        mesh=mesh,
        in_specs=(
            P(both, None, None),
            P(both, None, None),
            P(both, None),
            P(both, None, None),
            P(both),
            P(both, None, None),
            P(both, None, None),
            P(both, None),
        ),
        out_specs=P(both, None, None),
        check_vma=False,
    )
```

```python
import functools

import jax
import jax.numpy as jnp
from jax import lax
from jax.experimental import pallas as pl
from jax.experimental.pallas import tpu as pltpu
from jax.sharding import PartitionSpec as P

LEVELS = 6
ROUNDS = 5
CAP = 16
BLOCKS = 48
GROUP = 16
UPW = 4
ZS, XS = 8, 4
PEERS = XS * ZS
OFFSETS = (0, -1, 1, -2, 2)
NEAR = len(OFFSETS)
ORDER = (2, 1, 3, 0)
ZERO = LEVELS * CAP
ARRIVED = ZERO + 1
STORE = ARRIVED + 2 * ROUNDS * PEERS
T_BLOCK, T_REF, T_SLOT, T_SEND, T_ROWS = 0, 1, 5, 8, 24
E_ROW1 = 2 * XS * NEAR
E_ROW2 = E_ROW1 + 4 * XS
ENTRIES = E_ROW2 + 2 * XS
MESH = pl.DeviceIdType.MESH
ROWS = 8
LANES = 128
PARTS = 4
WIDTH = LANES // PARTS
SLOTS = ROUNDS * PARTS
LAG = 6


def groups_of(rows):
    return lax.broadcasted_iota(jnp.int32, (rows, LANES), 1) // WIDTH


def pick(group, values):
    result = values[PARTS - 1]
    for g in range(PARTS - 2, -1, -1):
        result = jnp.where(group == g, values[g], result)
    return result


def turns(value):
    return [value] + [pltpu.roll(value, WIDTH * t, 1) for t in range(1, PARTS)]


def make_table(z, level_ref, upwind_ref, send_in_ref, send_down_ref, table):
    square = (BLOCKS, BLOCKS)
    wide = (BLOCKS, LANES)
    row, col = (lax.broadcasted_iota(jnp.int32, square, d) for d in range(2))

    def down(mask, value):
        return jnp.sum(jnp.where(mask, value, 0), axis=0, keepdims=True)

    def upright(value):
        return jnp.sum(
            jnp.where(row == col, jnp.broadcast_to(value, square), 0), axis=1, keepdims=True
        )

    level = level_ref[...]
    level_col = upright(level)
    same = jnp.broadcast_to(level, square) == level_col
    rank_col = jnp.sum(jnp.where(same & (col < row), 1, 0), axis=1, keepdims=True)
    slot_col = level_col * CAP + rank_col
    table[...] = jnp.zeros(table.shape, jnp.int32)
    table[T_SLOT : T_SLOT + 1, :BLOCKS] = down(row == col, slot_col)
    here = slot_col == lax.broadcasted_iota(jnp.int32, wide, 1)
    table[T_BLOCK : T_BLOCK + 1, :] = down(here, lax.broadcasted_iota(jnp.int32, wide, 0))
    for j in range(UPW):
        t = upwind_ref[j : j + 1, :]
        local = ZERO + down(t == row, slot_col - ZERO)
        number = jnp.maximum(t - (BLOCKS + 1), 0)
        owner_z = number & (ZS - 1)
        away = (owner_z - z + ZS) & (ZS - 1)
        spot = jnp.zeros_like(away)
        for place, o in enumerate(OFFSETS + (3, 4, -3)):
            spot = jnp.where(away == o % ZS, place, spot)
        remote = ARRIVED + number - owner_z + spot
        ref = jnp.where(t <= BLOCKS, local, remote)
        table[T_REF + j : T_REF + j + 1, :] = ZERO + down(here, upright(ref) - ZERO)
    local_id = lax.broadcasted_iota(jnp.int32, (BLOCKS, PEERS), 0)
    for way, sent in enumerate((send_in_ref, send_down_ref)):
        for r in range(ROUNDS):
            place = T_SEND + way * ROUNDS + r
            table[place : place + 1, :PEERS] = CAP + down(sent[r] == local_id, rank_col - CAP)


def kernel(
    sections,
    level_ref,
    upwind_ref,
    send_in_ref,
    send_down_ref,
    residual,
    kin_ref,
    weight,
    frac,
    out,
    table,
    around,
    tab,
    tabs,
    kin,
    rights,
    factors,
    store,
    near,
    packs,
    arrived,
    sendb,
    pack_send,
    pack_recv,
    uni_send,
    uni_recv,
    tab_send,
    tab_recv,
    tab_local,
):
    sec = lax.axis_index("section")
    me = lax.axis_index("blk")
    x, z = me // ZS, lax.rem(me, ZS)
    has_next = sec < sections - 1
    has_prev = sec > 0
    columns = [lax.rem(x + xo, XS) * ZS for xo in range(XS)]
    rows = {zo: lax.rem(z + zo + ZS, ZS) for zo in range(-2, 3)}
    barrier = pltpu.get_barrier_semaphore()
    zeros = jnp.zeros((ROWS, LANES), jnp.float32)

    def at(section, xo, zo):
        return {"section": section, "blk": columns[xo] + rows[zo]}

    for xo in range(XS):
        for zo in range(-2, 3):
            if xo or zo:
                pl.semaphore_signal(
                    barrier, inc=1, device_id=at(sec, xo, zo), device_id_type=MESH
                )

    @pl.when(has_prev)
    def _():
        for xo in range(XS):
            for zo in range(-2, 3):
                pl.semaphore_signal(
                    barrier, inc=1, device_id=at(sec - 1, xo, zo), device_id_type=MESH
                )

    group = groups_of(ROWS)

    def prepare(parts, b):
        whole = residual[b]
        turned = [turns(whole[g * ROWS : (g + 1) * ROWS]) for g in range(PARTS)]
        scales = turns(jnp.concatenate([frac[b], weight[b], weight[b], frac[b][:2]], axis=0))
        for part in parts:
            rights[part, b] = pick(
                group, [turned[g][(g - part) % PARTS] for g in range(PARTS)]
            )
            factors[part, b] = pick(
                group, [scales[(g - part) % PARTS] for g in range(PARTS)]
            )

    def prepare_first(b, _):
        exact = kin_ref[b]
        coarse = exact.astype(jnp.bfloat16).astype(jnp.float32)
        kin[b] = jnp.concatenate([coarse, exact - coarse, coarse], axis=1).astype(jnp.bfloat16)
        prepare((0,), b)
        return 0

    def prepare_rest(b, _):
        prepare(range(1, PARTS), b)
        return 0

    def solve(part, level, slot, last=False):
        def gather(k):
            place = level * CAP + k
            b = tab[T_BLOCK, place]
            inflow = rights[part, b]
            factor = factors[part, b]
            for j in range(UPW):
                source = store[part, tab[T_REF + j, place]]
                inflow = inflow + factor[j : j + 1, :] * source
            turned = turns(inflow)
            all_species = jnp.concatenate(
                [
                    pick(group, [turned[(to - g) % PARTS] for to in range(PARTS)])
                    for g in range(PARTS)
                ],
                axis=0,
            )
            coarse = all_species.astype(jnp.bfloat16)
            rest = (all_species - coarse.astype(jnp.float32)).astype(jnp.bfloat16)
            return b, factor[UPW : UPW + 1, :], jnp.concatenate([coarse, coarse, rest], axis=0)

        def batch(i, _):
            spots = [i * GROUP + k for k in range(GROUP)]
            gathered = [gather(k) for k in spots]
            mixed = [
                jnp.dot(kin[b], terms, preferred_element_type=jnp.float32)
                for b, _, terms in gathered
            ]
            solved = [
                scale * pick(group, [m[g * ROWS : (g + 1) * ROWS] for g in range(PARTS)])
                for (_, scale, _), m in zip(gathered, mixed)
            ]
            for k, value in zip(spots, solved):
                store[part, level * CAP + k] = value
                if not last:
                    packs[slot, k] = value
                    near[part, k] = value
            return 0

        lax.fori_loop(0, CAP // GROUP, batch, 0)

    def pack_copy(slot, source, target, zo):
        return pltpu.make_async_remote_copy(
            src_ref=packs.at[slot, pl.ds(source * CAP, CAP)],
            dst_ref=packs.at[slot, pl.ds(target * CAP, CAP)],
            send_sem=pack_send.at[slot],
            recv_sem=pack_recv.at[slot, target],
            device_id=at(sec, 0, zo),
            device_id_type=MESH,
        )

    def pack_wait(slot, p):
        some = packs.at[slot, pl.ds(p * CAP, CAP)]
        pltpu.make_async_copy(some, some, pack_recv.at[slot, p]).wait()

    def hold(slot, p):
        part = lax.rem(slot, PARTS)
        for k in range(CAP):
            near[part, p * (CAP + 1) + k] = packs[slot, p * CAP + k]

    def fill(slot, entry, way, p, xo, zo):
        level, part = slot // PARTS, lax.rem(slot, PARTS)
        chosen = tabs[p, way * ROUNDS + level, columns[xo] + rows[zo]]
        sendb[slot, entry] = near[part, p * (CAP + 1) + chosen]

    def copy(slot, entry, count, way, place, xo, zo):
        return pltpu.make_async_remote_copy(
            src_ref=sendb.at[slot, pl.ds(entry, count)],
            dst_ref=arrived.at[way, slot, pl.ds(x * ZS + place, count)],
            send_sem=uni_send.at[way, slot],
            recv_sem=uni_recv.at[way, slot],
            device_id=at(sec + way, xo, zo),
            device_id_type=MESH,
        )

    def to_row(slot, way, xo, first, count):
        entry = (way * XS + xo) * NEAR
        for p in range(first, first + count):
            fill(slot, entry + p, way, p, xo, 0)
        if way or xo:
            copy(slot, entry + first, count, way, first, xo, 0).start()

    def to_columns(send_way):
        for xo in ORDER:
            send_way(xo, 0)

        @pl.when(has_next)
        def _():
            for xo in ORDER:
                send_way(xo, 1)

    def send_own(slot):
        pack_copy(slot, 0, 1, 1).start()
        pack_copy(slot, 0, 2, -1).start()

    def forward(slot):
        pack_wait(slot, 1)
        pack_copy(slot, 1, 3, 1).start()
        pack_wait(slot, 2)
        pack_copy(slot, 2, 4, -1).start()
        hold(slot, 1)
        hold(slot, 2)
        to_columns(lambda xo, way: to_row(slot, way, xo, 0, 3))

    def deliver(slot):
        for p in (3, 4):
            pack_wait(slot, p)
            hold(slot, p)

        def send_way(xo, way):
            far = E_ROW2 + way * XS + xo
            p, zo = ((3, 2), (4, -2))[way]
            fill(slot, far, way, p, xo, zo)
            copy(slot, far, 1, way, 6, xo, zo).start()
            up = E_ROW1 + way * XS + xo
            fill(slot, up, way, 3, xo, 1)
            copy(slot, up, 1, way, 7, xo, 1).start()
            down = E_ROW1 + (2 + way) * XS + xo
            fill(slot, down, way, 4, xo, -1)
            copy(slot, down, 1, way, 5, xo, -1).start()
            to_row(slot, way, xo, 3, 2)

        to_columns(send_way)

    def absorb(slot):
        level, part = slot // PARTS, lax.rem(slot, PARTS)
        some = arrived.at[0, slot, pl.ds(0, PEERS - NEAR)]
        pltpu.make_async_copy(some, some, uni_recv.at[0, slot]).wait()
        base = ARRIVED + level * PEERS
        for i in range(PEERS):
            store[part, base + i] = arrived[0, slot, i]
        for p in range(NEAR):
            store[part, base + x * ZS + p] = sendb[slot, p]

        @pl.when(has_prev)
        def _():
            every = arrived.at[1, slot]
            pltpu.make_async_copy(every, every, uni_recv.at[1, slot]).wait()
            for i in range(PEERS):
                store[part, base + ROUNDS * PEERS + i] = arrived[1, slot, i]

    make_table(z, level_ref, upwind_ref, send_in_ref, send_down_ref, table)
    moves = [
        pltpu.make_async_copy(table, tab, tab_local.at[NEAR]),
        pltpu.make_async_copy(table.at[pl.ds(T_SEND, 16)], tabs.at[0], tab_local.at[0]),
    ]
    for move in moves:
        move.start()
    lax.fori_loop(0, BLOCKS, prepare_first, 0, unroll=8)
    for part in range(PARTS):
        store[part, ZERO] = zeros
        for p in range(NEAR):
            near[part, p * (CAP + 1) + CAP] = zeros

    @pl.when(jnp.logical_not(has_prev))
    def _():
        def blank(i, _):
            for part in range(PARTS):
                store[part, ARRIVED + ROUNDS * PEERS + i] = zeros
            return 0

        lax.fori_loop(0, ROUNDS * PEERS, blank, 0)

    for move in moves:
        move.wait()
    solve(0, 0, 0)

    @pl.when(has_next)
    def _():
        pl.semaphore_wait(barrier, 2 * XS * NEAR - 1)

    @pl.when(jnp.logical_not(has_next))
    def _():
        pl.semaphore_wait(barrier, XS * NEAR - 1)

    send_own(0)
    for o in OFFSETS[1:]:
        p = OFFSETS.index(-o)
        pltpu.make_async_remote_copy(
            src_ref=table.at[pl.ds(T_SEND, 16)],
            dst_ref=around.at[p],
            send_sem=tab_send,
            recv_sem=tab_recv.at[p],
            device_id=at(sec, 0, o),
            device_id_type=MESH,
        ).start()
    lax.fori_loop(0, BLOCKS, prepare_rest, 0, unroll=8)

    def first(part, _):
        solve(part, 0, part)
        send_own(part)
        return 0

    lax.fori_loop(1, PARTS, first, 0)
    moves = []
    for p in range(1, NEAR):
        source = around.at[p]
        pltpu.make_async_copy(source, source, tab_recv.at[p]).wait()
        moves.append(pltpu.make_async_copy(source, tabs.at[p], tab_local.at[p]))
        moves[-1].start()
    for move in moves:
        move.wait()
    forward(0)

    def finish(slot, _):
        some = packs.at[slot, pl.ds(0, 4 * CAP)]
        pltpu.make_async_copy(some, some, pack_send.at[slot]).wait()
        some = sendb.at[slot, pl.ds(0, PEERS - NEAR)]
        pltpu.make_async_copy(some, some, uni_send.at[0, slot]).wait()

        @pl.when(has_next)
        def _():
            some = sendb.at[slot, pl.ds(0, PEERS)]
            pltpu.make_async_copy(some, some, uni_send.at[1, slot]).wait()

        return 0

    def step(slot, _):
        @pl.when(slot >= PARTS)
        def _():
            absorb(slot - PARTS)
            solve(lax.rem(slot, PARTS), slot // PARTS, slot)
            send_own(slot)

        forward(slot - 1)
        deliver(slot - 2)

        @pl.when(slot >= LAG)
        def _():
            finish(slot - LAG, 0)

        return 0

    lax.fori_loop(2, SLOTS, step, 0)
    absorb(SLOTS - PARTS)
    solve(0, ROUNDS, 0, last=True)
    forward(SLOTS - 1)
    deliver(SLOTS - 2)
    absorb(SLOTS - PARTS + 1)
    solve(1, ROUNDS, 0, last=True)
    deliver(SLOTS - 1)

    def tail(part, _):
        absorb(SLOTS - PARTS + part)
        solve(part, ROUNDS, 0, last=True)
        return 0

    lax.fori_loop(2, PARTS, tail, 0)

    def give(b, _):
        place = tab[T_SLOT, b]
        turned = [turns(store[part, place]) for part in range(PARTS)]
        for g in range(PARTS):
            out[b, g * ROWS : (g + 1) * ROWS] = pick(
                group, [turned[part][(part - g) % PARTS] for part in range(PARTS)]
            )
        return 0

    lax.fori_loop(0, BLOCKS, give, 0, unroll=8)

    lax.fori_loop(SLOTS - LAG, SLOTS, finish, 0)
    some = around.at[pl.ds(0, NEAR - 1)]
    pltpu.make_async_copy(some, some, tab_send).wait()


def shards(
    residual, kin_inverse, cell_weight, upwind_frac, block_level, send_in, send_down, upwind_slot
):
    blocks, species, cells = residual.shape
    vmem = pl.BlockSpec(memory_space=pltpu.VMEM)
    piece = (ROWS, LANES)
    return pl.pallas_call(
        functools.partial(kernel, lax.axis_size("section")),
        out_shape=jax.ShapeDtypeStruct(residual.shape, jnp.float32),
        in_specs=[vmem] * 8,
        out_specs=vmem,
        scratch_shapes=[
            pltpu.VMEM((T_ROWS, LANES), jnp.int32),
            pltpu.VMEM((NEAR, 16, LANES), jnp.int32),
            pltpu.SMEM((T_ROWS, LANES), jnp.int32),
            pltpu.SMEM((NEAR, 16, LANES), jnp.int32),
            pltpu.VMEM((blocks, species, 3 * species), jnp.bfloat16),
            pltpu.VMEM((PARTS, BLOCKS, *piece), jnp.float32),
            pltpu.VMEM((PARTS, BLOCKS, *piece), jnp.float32),
            pltpu.VMEM((PARTS, STORE, *piece), jnp.float32),
            pltpu.VMEM((PARTS, NEAR * (CAP + 1), *piece), jnp.float32),
            pltpu.VMEM((SLOTS, NEAR * CAP, *piece), jnp.float32),
            pltpu.VMEM((2, SLOTS, PEERS, *piece), jnp.float32),
            pltpu.VMEM((SLOTS, ENTRIES, *piece), jnp.float32),
            pltpu.SemaphoreType.DMA((SLOTS,)),
            pltpu.SemaphoreType.DMA((SLOTS, NEAR)),
            pltpu.SemaphoreType.DMA((2, SLOTS)),
            pltpu.SemaphoreType.DMA((2, SLOTS)),
            pltpu.SemaphoreType.DMA,
            pltpu.SemaphoreType.DMA((NEAR,)),
            pltpu.SemaphoreType.DMA((NEAR + 1,)),
        ],
        compiler_params=pltpu.CompilerParams(
            collective_id=0, has_side_effects=True, vmem_limit_bytes=44 * 1024 * 1024
        ),
    )(
        block_level[None],
        upwind_slot.T,
        send_in.transpose(1, 0, 2),
        send_down.transpose(1, 0, 2),
        residual,
        kin_inverse,
        cell_weight[:, None, :],
        upwind_frac,
    )


def solution(mesh):
    both = ("section", "blk")
    return jax.shard_map(
        shards,
        mesh=mesh,
        in_specs=(
            P(both, None, None),
            P(both, None, None),
            P(both, None),
            P(both, None, None),
            P(both),
            P(both, None, None),
            P(both, None, None),
            P(both, None),
        ),
        out_specs=P(both, None, None),
        check_vma=False,
    )
```

```python
import functools

import jax
import jax.numpy as jnp
from jax import lax
from jax.experimental import pallas as pl
from jax.experimental.pallas import tpu as pltpu
from jax.sharding import PartitionSpec as P

LEVELS = 6
ROUNDS = 5
CAP = 16
BLOCKS = 48
GROUP = 16
UPW = 4
ZS, XS = 8, 4
PEERS = XS * ZS
OFFSETS = (0, -1, 1, -2, 2)
NEAR = len(OFFSETS)
ORDER = (2, 1, 3, 0)
ZERO = LEVELS * CAP
ARRIVED = ZERO + 1
STORE = ARRIVED + 2 * ROUNDS * PEERS
T_BLOCK, T_REF, T_SLOT, T_SEND, T_ROWS = 0, 1, 5, 8, 24
E_ROW1 = 2 * XS * NEAR
E_ROW2 = E_ROW1 + 4 * XS
ENTRIES = E_ROW2 + 2 * XS
MESH = pl.DeviceIdType.MESH
ROWS = 8
LANES = 128
PARTS = 4
WIDTH = LANES // PARTS
SLOTS = ROUNDS * PARTS
LAG = 6


def groups_of(rows):
    return lax.broadcasted_iota(jnp.int32, (rows, LANES), 1) // WIDTH


def pick(group, values):
    result = values[PARTS - 1]
    for g in range(PARTS - 2, -1, -1):
        result = jnp.where(group == g, values[g], result)
    return result


def turns(value):
    return [value] + [pltpu.roll(value, WIDTH * t, 1) for t in range(1, PARTS)]


def make_table(z, level_ref, upwind_ref, send_in_ref, send_down_ref, table):
    square = (BLOCKS, BLOCKS)
    wide = (BLOCKS, LANES)
    row, col = (lax.broadcasted_iota(jnp.int32, square, d) for d in range(2))

    def down(mask, value):
        return jnp.sum(jnp.where(mask, value, 0), axis=0, keepdims=True)

    def upright(value):
        return jnp.sum(
            jnp.where(row == col, jnp.broadcast_to(value, square), 0), axis=1, keepdims=True
        )

    level = level_ref[...]
    level_col = upright(level)
    same = jnp.broadcast_to(level, square) == level_col
    rank_col = jnp.sum(jnp.where(same & (col < row), 1, 0), axis=1, keepdims=True)
    slot_col = level_col * CAP + rank_col
    table[...] = jnp.zeros(table.shape, jnp.int32)
    table[T_SLOT : T_SLOT + 1, :BLOCKS] = down(row == col, slot_col)
    here = slot_col == lax.broadcasted_iota(jnp.int32, wide, 1)
    table[T_BLOCK : T_BLOCK + 1, :] = down(here, lax.broadcasted_iota(jnp.int32, wide, 0))
    for j in range(UPW):
        t = upwind_ref[j : j + 1, :]
        local = ZERO + down(t == row, slot_col - ZERO)
        number = jnp.maximum(t - (BLOCKS + 1), 0)
        owner_z = number & (ZS - 1)
        away = (owner_z - z + ZS) & (ZS - 1)
        spot = jnp.zeros_like(away)
        for place, o in enumerate(OFFSETS + (3, 4, -3)):
            spot = jnp.where(away == o % ZS, place, spot)
        remote = ARRIVED + number - owner_z + spot
        ref = jnp.where(t <= BLOCKS, local, remote)
        table[T_REF + j : T_REF + j + 1, :] = ZERO + down(here, upright(ref) - ZERO)
    local_id = lax.broadcasted_iota(jnp.int32, (BLOCKS, PEERS), 0)
    for way, sent in enumerate((send_in_ref, send_down_ref)):
        for r in range(ROUNDS):
            place = T_SEND + way * ROUNDS + r
            table[place : place + 1, :PEERS] = CAP + down(sent[r] == local_id, rank_col - CAP)


def kernel(
    sections,
    level_ref,
    upwind_ref,
    send_in_ref,
    send_down_ref,
    residual,
    kin_ref,
    weight,
    frac,
    out,
    table,
    around,
    tab,
    tabs,
    kin,
    rights,
    factors,
    store,
    near,
    packs,
    arrived,
    sendb,
    pack_send,
    pack_recv,
    uni_send,
    uni_recv,
    tab_send,
    tab_recv,
    tab_local,
):
    sec = lax.axis_index("section")
    me = lax.axis_index("blk")
    x, z = me // ZS, lax.rem(me, ZS)
    has_next = sec < sections - 1
    has_prev = sec > 0
    columns = [lax.rem(x + xo, XS) * ZS for xo in range(XS)]
    rows = {zo: lax.rem(z + zo + ZS, ZS) for zo in range(-2, 3)}
    barrier = pltpu.get_barrier_semaphore()
    zeros = jnp.zeros((ROWS, LANES), jnp.float32)

    def at(section, xo, zo):
        return {"section": section, "blk": columns[xo] + rows[zo]}

    for xo in range(XS):
        for zo in range(-2, 3):
            if xo or zo:
                pl.semaphore_signal(
                    barrier, inc=1, device_id=at(sec, xo, zo), device_id_type=MESH
                )

    @pl.when(has_prev)
    def _():
        for xo in range(XS):
            for zo in range(-2, 3):
                pl.semaphore_signal(
                    barrier, inc=1, device_id=at(sec - 1, xo, zo), device_id_type=MESH
                )

    group = groups_of(ROWS)

    def prepare(parts, b):
        whole = residual[b]
        turned = [turns(whole[g * ROWS : (g + 1) * ROWS]) for g in range(PARTS)]
        scales = turns(jnp.concatenate([frac[b], weight[b], weight[b], frac[b][:2]], axis=0))
        for part in parts:
            rights[part, b] = pick(
                group, [turned[g][(g - part) % PARTS] for g in range(PARTS)]
            )
            factors[part, b] = pick(
                group, [scales[(g - part) % PARTS] for g in range(PARTS)]
            )

    def prepare_first(b, _):
        exact = kin_ref[b]
        coarse = exact.astype(jnp.bfloat16).astype(jnp.float32)
        kin[b] = jnp.concatenate([coarse, exact - coarse, coarse], axis=1).astype(jnp.bfloat16)
        prepare((0,), b)
        return 0

    def prepare_rest(b, _):
        prepare(range(1, PARTS), b)
        return 0

    def solve(part, level, slot, last=False):
        def gather(k):
            place = level * CAP + k
            b = tab[T_BLOCK, place]
            inflow = rights[part, b]
            factor = factors[part, b]
            for j in range(UPW):
                source = store[part, tab[T_REF + j, place]]
                inflow = inflow + factor[j : j + 1, :] * source
            turned = turns(inflow)
            all_species = jnp.concatenate(
                [
                    pick(group, [turned[(to - g) % PARTS] for to in range(PARTS)])
                    for g in range(PARTS)
                ],
                axis=0,
            )
            coarse = all_species.astype(jnp.bfloat16)
            rest = (all_species - coarse.astype(jnp.float32)).astype(jnp.bfloat16)
            return b, factor[UPW : UPW + 1, :], jnp.concatenate([coarse, coarse, rest], axis=0)

        def batch(i, _):
            spots = [i * GROUP + k for k in range(GROUP)]
            gathered = [gather(k) for k in spots]
            mixed = [
                jnp.dot(kin[b], terms, preferred_element_type=jnp.float32)
                for b, _, terms in gathered
            ]
            solved = [
                scale * pick(group, [m[g * ROWS : (g + 1) * ROWS] for g in range(PARTS)])
                for (_, scale, _), m in zip(gathered, mixed)
            ]
            for k, value in zip(spots, solved):
                store[part, level * CAP + k] = value
                if not last:
                    packs[slot, k] = value
                    near[part, k] = value
            return 0

        lax.fori_loop(0, CAP // GROUP, batch, 0)

    def pack_copy(slot, source, target, zo):
        return pltpu.make_async_remote_copy(
            src_ref=packs.at[slot, pl.ds(source * CAP, CAP)],
            dst_ref=packs.at[slot, pl.ds(target * CAP, CAP)],
            send_sem=pack_send.at[slot],
            recv_sem=pack_recv.at[slot, target],
            device_id=at(sec, 0, zo),
            device_id_type=MESH,
        )

    def pack_wait(slot, p):
        some = packs.at[slot, pl.ds(p * CAP, CAP)]
        pltpu.make_async_copy(some, some, pack_recv.at[slot, p]).wait()

    def hold(slot, p):
        part = lax.rem(slot, PARTS)
        for k in range(CAP):
            near[part, p * (CAP + 1) + k] = packs[slot, p * CAP + k]

    def fill(slot, entry, way, p, xo, zo):
        level, part = slot // PARTS, lax.rem(slot, PARTS)
        chosen = tabs[p, way * ROUNDS + level, columns[xo] + rows[zo]]
        sendb[slot, entry] = near[part, p * (CAP + 1) + chosen]

    def copy(slot, entry, count, way, place, xo, zo):
        return pltpu.make_async_remote_copy(
            src_ref=sendb.at[slot, pl.ds(entry, count)],
            dst_ref=arrived.at[way, slot, pl.ds(x * ZS + place, count)],
            send_sem=uni_send.at[way, slot],
            recv_sem=uni_recv.at[way, slot],
            device_id=at(sec + way, xo, zo),
            device_id_type=MESH,
        )

    def to_row(slot, way, xo, first, count):
        entry = (way * XS + xo) * NEAR
        for p in range(first, first + count):
            fill(slot, entry + p, way, p, xo, 0)
        if way or xo:
            copy(slot, entry + first, count, way, first, xo, 0).start()

    def to_columns(send_way):
        for xo in ORDER:
            send_way(xo, 0)

        @pl.when(has_next)
        def _():
            for xo in ORDER:
                send_way(xo, 1)

    def send_own(slot):
        pack_copy(slot, 0, 1, 1).start()
        pack_copy(slot, 0, 2, -1).start()

    def forward(slot):
        pack_wait(slot, 1)
        pack_copy(slot, 1, 3, 1).start()
        pack_wait(slot, 2)
        pack_copy(slot, 2, 4, -1).start()

    def spread(slot):
        hold(slot, 1)
        hold(slot, 2)
        to_columns(lambda xo, way: to_row(slot, way, xo, 0, 3))

    def deliver(slot):
        for p in (3, 4):
            pack_wait(slot, p)
            hold(slot, p)

        def send_way(xo, way):
            far = E_ROW2 + way * XS + xo
            p, zo = ((3, 2), (4, -2))[way]
            fill(slot, far, way, p, xo, zo)
            copy(slot, far, 1, way, 6, xo, zo).start()
            up = E_ROW1 + way * XS + xo
            fill(slot, up, way, 3, xo, 1)
            copy(slot, up, 1, way, 7, xo, 1).start()
            down = E_ROW1 + (2 + way) * XS + xo
            fill(slot, down, way, 4, xo, -1)
            copy(slot, down, 1, way, 5, xo, -1).start()
            to_row(slot, way, xo, 3, 2)

        to_columns(send_way)

    def absorb(slot):
        level, part = slot // PARTS, lax.rem(slot, PARTS)
        some = arrived.at[0, slot, pl.ds(0, PEERS - NEAR)]
        pltpu.make_async_copy(some, some, uni_recv.at[0, slot]).wait()
        base = ARRIVED + level * PEERS
        for i in range(PEERS):
            store[part, base + i] = arrived[0, slot, i]
        for p in range(NEAR):
            store[part, base + x * ZS + p] = sendb[slot, p]

        @pl.when(has_prev)
        def _():
            every = arrived.at[1, slot]
            pltpu.make_async_copy(every, every, uni_recv.at[1, slot]).wait()
            for i in range(PEERS):
                store[part, base + ROUNDS * PEERS + i] = arrived[1, slot, i]

    make_table(z, level_ref, upwind_ref, send_in_ref, send_down_ref, table)
    moves = [
        pltpu.make_async_copy(table, tab, tab_local.at[NEAR]),
        pltpu.make_async_copy(table.at[pl.ds(T_SEND, 16)], tabs.at[0], tab_local.at[0]),
    ]
    for move in moves:
        move.start()
    lax.fori_loop(0, BLOCKS, prepare_first, 0, unroll=8)
    for part in range(PARTS):
        store[part, ZERO] = zeros
        for p in range(NEAR):
            near[part, p * (CAP + 1) + CAP] = zeros

    @pl.when(jnp.logical_not(has_prev))
    def _():
        def blank(i, _):
            for part in range(PARTS):
                store[part, ARRIVED + ROUNDS * PEERS + i] = zeros
            return 0

        lax.fori_loop(0, ROUNDS * PEERS, blank, 0)

    for move in moves:
        move.wait()
    solve(0, 0, 0)

    @pl.when(has_next)
    def _():
        pl.semaphore_wait(barrier, 2 * XS * NEAR - 1)

    @pl.when(jnp.logical_not(has_next))
    def _():
        pl.semaphore_wait(barrier, XS * NEAR - 1)

    send_own(0)
    for o in OFFSETS[1:]:
        p = OFFSETS.index(-o)
        pltpu.make_async_remote_copy(
            src_ref=table.at[pl.ds(T_SEND, 16)],
            dst_ref=around.at[p],
            send_sem=tab_send,
            recv_sem=tab_recv.at[p],
            device_id=at(sec, 0, o),
            device_id_type=MESH,
        ).start()
    lax.fori_loop(0, BLOCKS, prepare_rest, 0, unroll=8)

    def first(part, _):
        solve(part, 0, part)
        send_own(part)
        return 0

    lax.fori_loop(1, PARTS, first, 0)
    moves = []
    for p in range(1, NEAR):
        source = around.at[p]
        pltpu.make_async_copy(source, source, tab_recv.at[p]).wait()
        moves.append(pltpu.make_async_copy(source, tabs.at[p], tab_local.at[p]))
        moves[-1].start()
    for move in moves:
        move.wait()
    forward(0)
    spread(0)

    def finish(slot, _):
        some = packs.at[slot, pl.ds(0, 4 * CAP)]
        pltpu.make_async_copy(some, some, pack_send.at[slot]).wait()
        some = sendb.at[slot, pl.ds(0, PEERS - NEAR)]
        pltpu.make_async_copy(some, some, uni_send.at[0, slot]).wait()

        @pl.when(has_next)
        def _():
            some = sendb.at[slot, pl.ds(0, PEERS)]
            pltpu.make_async_copy(some, some, uni_send.at[1, slot]).wait()

        return 0

    def step(slot, _):
        @pl.when(slot >= PARTS)
        def _():
            absorb(slot - PARTS)
            solve(lax.rem(slot, PARTS), slot // PARTS, slot)
            send_own(slot)

        forward(slot - 1)
        deliver(slot - 2)
        spread(slot - 1)

        @pl.when(slot >= LAG)
        def _():
            finish(slot - LAG, 0)

        return 0

    lax.fori_loop(2, SLOTS, step, 0)
    absorb(SLOTS - PARTS)
    solve(0, ROUNDS, 0, last=True)
    forward(SLOTS - 1)
    deliver(SLOTS - 2)
    spread(SLOTS - 1)
    absorb(SLOTS - PARTS + 1)
    solve(1, ROUNDS, 0, last=True)
    deliver(SLOTS - 1)

    def tail(part, _):
        absorb(SLOTS - PARTS + part)
        solve(part, ROUNDS, 0, last=True)
        return 0

    lax.fori_loop(2, PARTS, tail, 0)

    def give(b, _):
        place = tab[T_SLOT, b]
        turned = [turns(store[part, place]) for part in range(PARTS)]
        for g in range(PARTS):
            out[b, g * ROWS : (g + 1) * ROWS] = pick(
                group, [turned[part][(part - g) % PARTS] for part in range(PARTS)]
            )
        return 0

    lax.fori_loop(0, BLOCKS, give, 0, unroll=8)

    lax.fori_loop(SLOTS - LAG, SLOTS, finish, 0)
    some = around.at[pl.ds(0, NEAR - 1)]
    pltpu.make_async_copy(some, some, tab_send).wait()


def shards(
    residual, kin_inverse, cell_weight, upwind_frac, block_level, send_in, send_down, upwind_slot
):
    blocks, species, cells = residual.shape
    vmem = pl.BlockSpec(memory_space=pltpu.VMEM)
    piece = (ROWS, LANES)
    return pl.pallas_call(
        functools.partial(kernel, lax.axis_size("section")),
        out_shape=jax.ShapeDtypeStruct(residual.shape, jnp.float32),
        in_specs=[vmem] * 8,
        out_specs=vmem,
        scratch_shapes=[
            pltpu.VMEM((T_ROWS, LANES), jnp.int32),
            pltpu.VMEM((NEAR, 16, LANES), jnp.int32),
            pltpu.SMEM((T_ROWS, LANES), jnp.int32),
            pltpu.SMEM((NEAR, 16, LANES), jnp.int32),
            pltpu.VMEM((blocks, species, 3 * species), jnp.bfloat16),
            pltpu.VMEM((PARTS, BLOCKS, *piece), jnp.float32),
            pltpu.VMEM((PARTS, BLOCKS, *piece), jnp.float32),
            pltpu.VMEM((PARTS, STORE, *piece), jnp.float32),
            pltpu.VMEM((PARTS, NEAR * (CAP + 1), *piece), jnp.float32),
            pltpu.VMEM((SLOTS, NEAR * CAP, *piece), jnp.float32),
            pltpu.VMEM((2, SLOTS, PEERS, *piece), jnp.float32),
            pltpu.VMEM((SLOTS, ENTRIES, *piece), jnp.float32),
            pltpu.SemaphoreType.DMA((SLOTS,)),
            pltpu.SemaphoreType.DMA((SLOTS, NEAR)),
            pltpu.SemaphoreType.DMA((2, SLOTS)),
            pltpu.SemaphoreType.DMA((2, SLOTS)),
            pltpu.SemaphoreType.DMA,
            pltpu.SemaphoreType.DMA((NEAR,)),
            pltpu.SemaphoreType.DMA((NEAR + 1,)),
        ],
        compiler_params=pltpu.CompilerParams(
            collective_id=0, has_side_effects=True, vmem_limit_bytes=44 * 1024 * 1024
        ),
    )(
        block_level[None],
        upwind_slot.T,
        send_in.transpose(1, 0, 2),
        send_down.transpose(1, 0, 2),
        residual,
        kin_inverse,
        cell_weight[:, None, :],
        upwind_frac,
    )


def solution(mesh):
    both = ("section", "blk")
    return jax.shard_map(
        shards,
        mesh=mesh,
        in_specs=(
            P(both, None, None),
            P(both, None, None),
            P(both, None),
            P(both, None, None),
            P(both),
            P(both, None, None),
            P(both, None, None),
            P(both, None),
        ),
        out_specs=P(both, None, None),
        check_vma=False,
    )
```
